32 devices in a mesh: groups: 2 (over x), expert: 16 (over z, y, core).
Axes of the slice: x: 2, y: 2, z: 4, core: 2. Of those that a mesh axis runs over, the one named last changes fastest.
Arguments:
- activations: bfloat16 [16, 256, 1536], P('expert', 'groups'), parts along dimension 1, may hold values from -6 to 6
- routing: int32 [256, 6], P('groups'), parts along dimension 0, may hold values from 0 to 15, all different within a row
- pairs: int32 [16, 3], replicated, may hold values from -1 to 15, as said below
Outputs:
- energy: float32 [16, 6, 1536], P('expert', 'groups'), parts along dimension 1
The draws below stay inside these ranges and needn't reach their ends.
There are 2 independent parts, one for each index of `groups`. The reference program is written for one: setup_inputs(seed, part) draws one part's arguments, and reference() takes and returns one part's arrays. A program takes and returns all parts, laid end to end along the dimension named above; an argument that names none is the same for every part. Nothing has to cross between parts.
Inputs may be any that keep to these rules, and one draw needn't show every extreme that they name: `pairs`: experts fall into merge clusters of 8; each expert lists 1 to 3 distinct partners of its own cluster other than itself, used slots first and -1 after them; some expert uses all 3 slots and some only one.
All inputs are finite; a program needn't handle non-finite values.
Results may differ from the reference program's by a relative error of at most 0.0023.
Values may be sent and summed in bfloat16 or wider, within the bound.
A program may use at most 64 MiB of HBM per device.

```python
import jax
import jax.numpy as jnp
from jax import lax

H = 1536
TOPK = 6
PMAX = 3
CLUSTER = 8
EXPERTS = 16
TOKENS = 128


def draw_pairs(key, part):
    key = jax.random.fold_in(key, 11)
    key_order, key_offs, key_count, key_full = jax.random.split(key, 4)
    order = jax.random.permutation(key_order, EXPERTS).astype(jnp.int32)
    places = jnp.zeros((EXPERTS,), jnp.int32).at[order].set(jnp.arange(EXPERTS, dtype=jnp.int32))
    cluster = places // CLUSTER
    within = places % CLUSTER
    scores = jax.random.randint(key_offs, (EXPERTS, CLUSTER - 1), 0, 2 ** 20) * CLUSTER + jnp.arange(CLUSTER - 1, dtype=jnp.int32)[None, :]
    offsets = jnp.argsort(scores, axis=1, stable=True)[:, :PMAX].astype(jnp.int32) + 1
    partner = order[cluster[:, None] * CLUSTER + (within[:, None] + offsets) % CLUSTER]
    counts = jax.random.randint(key_count, (EXPERTS,), 1, PMAX + 1)
    fullest = jax.random.randint(key_full, (), 0, EXPERTS)
    indices = jnp.arange(EXPERTS, dtype=jnp.int32)
    counts = jnp.where(indices == fullest, PMAX, counts)
    counts = jnp.where(indices == (fullest + 1) % EXPERTS, 1, counts)
    used = jnp.arange(PMAX, dtype=jnp.int32)[None, :] < counts[:, None]
    return jnp.where(used, partner, -1).astype(jnp.int32)


def level_of(own_key, extent, cuts, low, top_value):
    gain = 1.0
    for axis_at, blocks in cuts:
        draws = jax.random.uniform(jax.random.fold_in(jax.random.fold_in(own_key, 6), axis_at), (blocks,), jnp.float32, low / len(cuts), top_value / len(cuts))
        gain = gain * jnp.repeat(jnp.exp(draws), extent[axis_at] // blocks).reshape((-1,) + (1,) * (len(extent) - 1 - axis_at))
    return gain


def distinct(stream_key, rows, number_of, top, lift):
    sequence = jax.random.permutation(jax.random.fold_in(stream_key, 1), number_of)
    pull = sequence
    for power in range(3):
        pull = pull * pull // number_of
    pull = pull * lift // number_of
    tickets = jax.random.randint(jax.random.fold_in(stream_key, 2), (rows, number_of), 0, 4096) + pull
    sure = jax.random.permutation(jax.random.fold_in(stream_key, 3), rows)[jnp.arange(number_of) % rows]
    tickets = jnp.where(jnp.arange(rows)[:, None] == sure[None, :], 1 << 14, tickets)
    priority = tickets * number_of + jnp.arange(number_of)
    return lax.top_k(priority.astype(jnp.int32), top)[1].astype(jnp.int32)


def centred(rng, dims, scale, most, cuts=(), held_as=jnp.bfloat16):
    array = scale * jax.random.normal(rng, dims, jnp.float32)
    if cuts:
        array = array * level_of(rng, dims, cuts, -0.22, 0.18)
    return jnp.clip(array, -most, most).astype(held_as)


def setup_inputs(seed: int = 0, part: int = 0) -> dict:
    key_list = jax.random.split(jax.random.key(seed), 4)
    part_splits = jax.random.split(jax.random.fold_in(key_list[3], part), 4)
    activations = centred(part_splits[0], (EXPERTS, TOKENS, H), 1.0, 6.0, ((0, 16),))
    routing = distinct(part_splits[1], TOKENS, EXPERTS, TOPK, 6144)
    pairs = draw_pairs(jax.random.fold_in(key_list[3], 71), part)
    return {"activations": activations, "routing": routing, "pairs": pairs}


def token_weights(routing):
    experts = jnp.arange(EXPERTS, dtype=jnp.int32)
    hit = jnp.any(routing[:, :, None] == experts[None, None, :], axis=1)
    return 0.5 + 1.5 * hit.astype(jnp.float32)

def normed(values, weights, total):
    values = values.astype(jnp.float32)
    center = lax.optimization_barrier(jnp.sum(weights[:, None] * values, axis=0)) / total
    shifted = values - center[None, :]
    spread = lax.optimization_barrier(jnp.sum(weights[:, None] * shifted * shifted, axis=0)) / total
    scale = jnp.sqrt(weights / total)[:, None]
    return (shifted * scale / jnp.sqrt(spread[None, :] + 1e-06)).astype(jnp.bfloat16)

def reference(activations, routing, pairs):
    table = token_weights(routing)

    def one_expert(index):
        own = activations[index]
        own_w = table[:, index]
        results = []
        for slot in range(PMAX):
            partner = pairs[index, slot]
            valid = (partner >= 0).astype(jnp.float32)
            safe = jnp.maximum(partner, 0)
            other = activations[safe]
            weights = own_w * table[:, safe] * valid
            total = jnp.sum(weights)
            total = jnp.where(total > 0, total, 1.0)
            left = normed(own, weights, total)
            right = normed(other, weights, total)
            corr = jnp.dot(left.T, right, preferred_element_type=jnp.float32)
            results.append(lax.optimization_barrier(jnp.sum(corr * corr, axis=1)))
        return jnp.stack(results, axis=0)
    return lax.map(one_expert, jnp.arange(EXPERTS, dtype=jnp.int32))
```

```python
import functools

import jax
import jax.numpy as jnp
from jax import lax
from jax.experimental import pallas as pl
from jax.experimental.pallas import tpu as pltpu
from jax.sharding import PartitionSpec as P

F32 = jnp.float32
BF16 = jnp.bfloat16
CHUNK = 256


def gram_kernel(
    experts, x_ref, routing_ref, pairs_ref, out_ref,
    z_ref, wt_ref, send_ref, recv_ref, mean_ref, rate_ref, send_sem, recv_sem,
):
    me = lax.axis_index("expert")
    tokens, width = x_ref.shape
    slots = wt_ref.shape[0]

    barrier = pltpu.get_barrier_semaphore()
    for s in range(1, experts):
        pl.semaphore_signal(
            barrier, inc=1, device_id={"expert": lax.rem(me + s, experts)},
            device_id_type=pl.DeviceIdType.MESH,
        )

    lane = lax.broadcasted_iota(jnp.int32, (tokens, 128), 1)
    label = lax.rem(lane + me, experts)
    hit = jnp.zeros((tokens, 128), jnp.bool_)
    mine = jnp.zeros((tokens, 1), jnp.bool_)
    for k in range(routing_ref.shape[1]):
        chosen = routing_ref[:, k:k + 1]
        hit = hit | (chosen == label)
        mine = mine | (chosen == me)
    g = jnp.where(hit, 2.0, 0.5)
    g_me = jnp.where(mine, 2.0, 0.5)
    w = jnp.where(lane == 0, 1.0, g * g_me)
    wt = w.T[:slots, :]
    wt_ref[...] = wt
    total = jnp.sum(wt, axis=1, keepdims=True)
    wt16 = wt.astype(BF16)

    for c in range(0, width, CHUNK):
        cols = slice(c, c + CHUNK)
        x = x_ref[:, cols]
        mean = jnp.dot(wt16, x, preferred_element_type=F32) / total
        center = mean[0:1, :]
        y = x.astype(F32) - center
        sq = y * y
        high = sq.astype(BF16)
        low = (sq - high.astype(F32)).astype(BF16)
        second = (
            jnp.dot(wt16, high, preferred_element_type=F32)
            + jnp.dot(wt16, low, preferred_element_type=F32)
        ) / total
        moved = mean - center
        var = jnp.maximum(second - moved * moved, 0.0)
        mean_ref[:, cols] = mean
        rate_ref[:, cols] = 1.0 / (jnp.sqrt(var + 1e-06) * jnp.sqrt(total))

    pl.semaphore_wait(barrier, experts - 1)

    copies = []
    for s in range(1, experts):
        gram = jnp.zeros((tokens, tokens), F32)
        for c in range(0, width, CHUNK):
            cols = slice(c, c + CHUNK)
            z = ((x_ref[:, cols].astype(F32) - mean_ref[s:s + 1, cols]) * rate_ref[s:s + 1, cols]).astype(BF16)
            z_ref[s, :, cols] = z
            gram += lax.dot_general(z, z, (((1,), (1,)), ((), ())), preferred_element_type=F32)
        send_ref[s] = (gram * w[:, s:s + 1] * wt_ref[s:s + 1, :]).astype(BF16)
        copy = pltpu.make_async_remote_copy(
            src_ref=send_ref.at[s],
            dst_ref=recv_ref.at[s],
            send_sem=send_sem.at[s],
            recv_sem=recv_sem.at[s],
            device_id={"expert": lax.rem(me + s, experts)},
            device_id_type=pl.DeviceIdType.MESH,
        )
        copy.start()
        copies.append(copy)
    for copy in copies:
        copy.wait()

    for p in range(pairs_ref.shape[1]):
        partner = pairs_ref[me, p]
        used = partner >= 0
        other = jnp.where(used, partner, lax.rem(me + 1, experts))
        ahead = lax.rem(other - me + experts, experts)
        behind = lax.rem(me - other + experts, experts)
        gram = recv_ref[behind]
        keep = jnp.where(used, 1.0, 0.0).astype(F32)
        for c in range(0, width, CHUNK):
            cols = slice(c, c + CHUNK)
            z = z_ref[ahead, :, cols]
            product = jnp.dot(gram, z, preferred_element_type=F32)
            out_ref[p:p + 1, cols] = jnp.sum(product * z.astype(F32), axis=0, keepdims=True) * keep


def gram_device(activations, routing, pairs):
    experts = lax.axis_size("expert")
    own = activations[0]
    tokens, width = own.shape
    count = pairs.shape[1]
    slots = -(-experts // 8) * 8
    vmem = pl.BlockSpec(memory_space=pltpu.VMEM)
    result = pl.pallas_call(
        functools.partial(gram_kernel, experts),
        out_shape=jax.ShapeDtypeStruct((count, width), F32),
        in_specs=[vmem, vmem, pl.BlockSpec(memory_space=pltpu.SMEM)],
        out_specs=vmem,
        scratch_shapes=[
            pltpu.VMEM((experts, tokens, width), BF16),
            pltpu.VMEM((slots, tokens), F32),
            pltpu.VMEM((experts, tokens, tokens), BF16),
            pltpu.VMEM((experts, tokens, tokens), BF16),
            pltpu.VMEM((slots, width), F32),
            pltpu.VMEM((slots, width), F32),
            pltpu.SemaphoreType.DMA((experts,)),
            pltpu.SemaphoreType.DMA((experts,)),
        ],
        compiler_params=pltpu.CompilerParams(
            collective_id=0, has_side_effects=True, vmem_limit_bytes=32 * 1024 * 1024
        ),
    )(own, routing, pairs)
    return result[None]


def weights_for(routing, experts):
    labels = jnp.arange(experts, dtype=jnp.int32)
    hit = jnp.any(routing[:, :, None] == labels[None, None, :], axis=1)
    return 0.5 + 1.5 * hit.astype(jnp.float32)


def normed(values, weights, total):
    values = values.astype(jnp.float32)
    center = jnp.sum(weights[:, None] * values, axis=0) / total
    shifted = values - center[None, :]
    spread = jnp.sum(weights[:, None] * shifted * shifted, axis=0) / total
    scale = jnp.sqrt(weights / total)[:, None]
    return (shifted * scale / jnp.sqrt(spread[None, :] + 1e-06)).astype(jnp.bfloat16)


def energies(own, own_w, blocks, partner_w):
    count = blocks.shape[0]
    tokens = own.shape[0]
    width = own.shape[1]
    other = blocks.reshape(count, tokens, width)
    part_w = partner_w.reshape(count, tokens)

    def one_slot(items):
        weights = own_w * items[1].astype(jnp.float32)
        total = jnp.sum(weights)
        total = jnp.where(total > 0, total, 1.0)
        left = normed(own, weights, total)
        right = normed(items[0], weights, total)
        corr = jnp.dot(left.T, right, preferred_element_type=jnp.float32)
        return jnp.sum(corr * corr, axis=1)

    return lax.map(one_slot, (other, part_w))


def slice_device(activations, routing, pairs):
    own = activations[0]
    experts = lax.axis_size("expert")
    me = lax.axis_index("expert")
    tokens = own.shape[0]
    width = own.shape[1]
    piece = tokens // experts
    columns = lax.all_to_all(
        own.reshape(experts, piece, width), "expert", split_axis=0, concat_axis=0, tiled=True
    )
    local_rows = lax.dynamic_slice_in_dim(routing, me * piece, piece, 0)
    local_table = weights_for(local_rows, experts)
    valid = (pairs >= 0).astype(jnp.float32)
    safe = jnp.maximum(pairs, 0).T
    send_blocks = columns[safe]
    send_weights = (local_table.T[safe] * valid.T[:, :, None]).astype(jnp.bfloat16)
    own_w = 0.5 + 1.5 * jnp.any(routing == me, axis=1).astype(jnp.float32)
    result = energies(
        own,
        own_w,
        lax.all_to_all(send_blocks, "expert", split_axis=1, concat_axis=1, tiled=True),
        lax.all_to_all(send_weights, "expert", split_axis=1, concat_axis=1, tiled=True),
    )
    return result[None]


def per_device(activations, routing, pairs):
    experts = lax.axis_size("expert")
    tokens, width = activations.shape[1:]
    gram_sends = experts * tokens * tokens
    slice_sends = (1 + pairs.shape[1]) * tokens * width
    if gram_sends < slice_sends:
        return gram_device(activations, routing, pairs)
    return slice_device(activations, routing, pairs)


def solution(mesh):
    return jax.shard_map(
        per_device,
        mesh=mesh,
        in_specs=(P("expert", "groups", None), P("groups", None), P()),
        out_specs=P("expert", "groups", None),
        check_vma=False,
    )
```

```python
import functools

import jax
import jax.numpy as jnp
from jax import lax
from jax.experimental import pallas as pl
from jax.experimental.pallas import tpu as pltpu
from jax.sharding import PartitionSpec as P

F32 = jnp.float32
BF16 = jnp.bfloat16
CHUNK = 256
AHEAD = 4


def gram_kernel(
    experts, order, x_hbm, routing_ref, pairs_ref, out_ref,
    x_ref, z_ref, wt_ref, send_ref, recv_ref, edge_ref, edge_in_ref, mean_ref, rate_ref,
    load_sem, send_sem, recv_sem, edge_sem, edge_in_sem,
):
    me = lax.axis_index("expert")
    tokens, width = x_ref.shape
    slots = wt_ref.shape[0]
    load = pltpu.make_async_copy(x_hbm, x_ref, load_sem.at[0])
    load.start()
    half = experts // 2 if experts % 2 == 0 else experts

    def split(index):
        upper = jnp.where(index >= half, 1, 0)
        return upper, index - upper * half

    def wrap(value, count):
        return jnp.where(value >= count, value - count, value)

    my_upper, my_place = split(me)

    def toward(s):
        upper, place = (s // half, s % half) if isinstance(s, int) else split(s)
        return wrap(my_upper + upper, 2) * half + wrap(my_place + place, half)

    def between(start, end):
        return wrap(end[0] - start[0] + 2, 2) * half + wrap(end[1] - start[1] + half, half)

    barrier = pltpu.get_barrier_semaphore()
    for s in range(1, experts):
        pl.semaphore_signal(
            barrier, inc=1, device_id={"expert": toward(s)},
            device_id_type=pl.DeviceIdType.MESH,
        )

    slot = lax.broadcasted_iota(jnp.int32, (slots, tokens), 0)
    label = toward(slot)
    hit = jnp.zeros((slots, tokens), jnp.bool_)
    mine = jnp.zeros((1, tokens), jnp.bool_)
    for k in range(routing_ref.shape[0]):
        chosen = routing_ref[k:k + 1, :]
        hit = hit | (chosen == label)
        mine = mine | (chosen == me)
    wt = jnp.where(slot == 0, 1.0, jnp.where(hit, 2.0, 0.5) * jnp.where(mine, 2.0, 0.5))
    wt_ref[...] = wt
    w = wt.T
    total = jnp.sum(wt, axis=1, keepdims=True)
    wt16 = wt.astype(BF16)

    load.wait()
    for c in range(0, width, CHUNK):
        cols = slice(c, c + CHUNK)
        x = x_ref[:, cols]
        mean = jnp.dot(wt16, x, preferred_element_type=F32) / total
        center = mean[0:1, :]
        y = x.astype(F32) - center
        sq = y * y
        high = sq.astype(BF16)
        low = (sq - high.astype(F32)).astype(BF16)
        second = (
            jnp.dot(wt16, high, preferred_element_type=F32)
            + jnp.dot(wt16, low, preferred_element_type=F32)
        ) / total
        moved = mean - center
        var = jnp.maximum(second - moved * moved, 0.0)
        mean_ref[:, cols] = mean
        rate_ref[:, cols] = 1.0 / (jnp.sqrt(var + 1e-06) * jnp.sqrt(total))

    mid = tokens // 2
    row = lax.broadcasted_iota(jnp.int32, (mid, tokens), 0)
    col = lax.broadcasted_iota(jnp.int32, (mid, tokens), 1)
    factor = jnp.where(row == col, 1.0, 2.0)

    copies = []

    def send(s):
        for source, target, out_sem, in_sem in (
            (send_ref, recv_ref, send_sem, recv_sem), (edge_ref, edge_in_ref, edge_sem, edge_in_sem)
        ):
            copy = pltpu.make_async_remote_copy(
                src_ref=source.at[s],
                dst_ref=target.at[s],
                send_sem=out_sem.at[s],
                recv_sem=in_sem.at[s],
                device_id={"expert": toward(s)},
                device_id_type=pl.DeviceIdType.MESH,
            )
            copy.start()
            copies.append(copy)

    for n, s in enumerate(order):
        for c in range(0, width, CHUNK):
            cols = slice(c, c + CHUNK)
            z_ref[s, :, cols] = (
                (x_ref[:, cols].astype(F32) - mean_ref[s:s + 1, cols]) * rate_ref[s:s + 1, cols]
            ).astype(BF16)
        z = z_ref[s]
        gram = lax.dot_general(z, z, (((1,), (1,)), ((), ())), preferred_element_type=F32)
        gram = gram * w[:, s:s + 1] * wt_ref[s:s + 1, :]
        top = gram[:mid, :] * factor
        below = pltpu.roll(gram[mid:, :], mid, 1)
        send_ref[s] = jnp.where(row <= col, top, below * 2.0).astype(BF16)
        edge_ref[s] = jnp.sum(jnp.where(row == col, below, 0.0), axis=0, keepdims=True)
        if n + 1 == AHEAD:
            pl.semaphore_wait(barrier, experts - 1)
            for earlier in order[:n]:
                send(earlier)
        if n + 1 >= AHEAD:
            send(s)
    for copy in copies:
        copy.wait()

    for p in range(pairs_ref.shape[0]):
        partner = pairs_ref[p, me]
        used = partner >= 0
        other = jnp.where(used, partner, toward(1))
        ahead = between((my_upper, my_place), split(other))
        behind = between(split(other), (my_upper, my_place))
        packed = recv_ref[behind].astype(F32)
        edge = jnp.where(row == col, edge_in_ref[behind], 0.0)
        lower = pltpu.roll(jnp.where(row > col, packed, edge), mid, 1)
        gram = jnp.concatenate([jnp.where(row <= col, packed, 0.0), lower], axis=0).astype(BF16)
        keep = jnp.where(used, 1.0, 0.0).astype(F32)
        for c in range(0, width, CHUNK):
            cols = slice(c, c + CHUNK)
            z = z_ref[ahead, :, cols]
            product = jnp.dot(gram, z, preferred_element_type=F32)
            out_ref[p, :, cols] = jnp.sum(product * z.astype(F32), axis=0, keepdims=True) * keep


def sending_order(experts):
    half = experts // 2
    far, near = list(range(half, experts)), list(range(1, half))
    return [s for pair in zip(far, near) for s in pair] + far[len(near):]


def gram_device(activations, routing, pairs):
    experts = lax.axis_size("expert")
    own = activations[0]
    tokens, width = own.shape
    count = pairs.shape[1]
    slots = -(-experts // 8) * 8
    order = sending_order(experts)
    vmem = pl.BlockSpec(memory_space=pltpu.VMEM)
    result = pl.pallas_call(
        functools.partial(gram_kernel, experts, order),
        out_shape=jax.ShapeDtypeStruct((count, 1, width), F32),
        in_specs=[pl.BlockSpec(memory_space=pltpu.HBM), vmem, pl.BlockSpec(memory_space=pltpu.SMEM)],
        out_specs=vmem,
        scratch_shapes=[
            pltpu.VMEM((tokens, width), BF16),
            pltpu.VMEM((experts, tokens, width), BF16),
            pltpu.VMEM((slots, tokens), F32),
            pltpu.VMEM((experts, tokens // 2, tokens), BF16),
            pltpu.VMEM((experts, tokens // 2, tokens), BF16),
            pltpu.VMEM((experts, 1, tokens), F32),
            pltpu.VMEM((experts, 1, tokens), F32),
            pltpu.VMEM((slots, width), F32),
            pltpu.VMEM((slots, width), F32),
            pltpu.SemaphoreType.DMA((width // CHUNK,)),
            pltpu.SemaphoreType.DMA((experts,)),
            pltpu.SemaphoreType.DMA((experts,)),
            pltpu.SemaphoreType.DMA((experts,)),
            pltpu.SemaphoreType.DMA((experts,)),
        ],
        compiler_params=pltpu.CompilerParams(
            collective_id=0, has_side_effects=True, vmem_limit_bytes=60 * 1024 * 1024
        ),
    )(own, routing.T, pairs.T)
    return result.reshape(1, count, width)


def weights_for(routing, experts):
    labels = jnp.arange(experts, dtype=jnp.int32)
    hit = jnp.any(routing[:, :, None] == labels[None, None, :], axis=1)
    return 0.5 + 1.5 * hit.astype(jnp.float32)


def normed(values, weights, total):
    values = values.astype(jnp.float32)
    center = jnp.sum(weights[:, None] * values, axis=0) / total
    shifted = values - center[None, :]
    spread = jnp.sum(weights[:, None] * shifted * shifted, axis=0) / total
    scale = jnp.sqrt(weights / total)[:, None]
    return (shifted * scale / jnp.sqrt(spread[None, :] + 1e-06)).astype(jnp.bfloat16)


def energies(own, own_w, blocks, partner_w):
    count = blocks.shape[0]
    tokens = own.shape[0]
    width = own.shape[1]
    other = blocks.reshape(count, tokens, width)
    part_w = partner_w.reshape(count, tokens)

    def one_slot(items):
        weights = own_w * items[1].astype(jnp.float32)
        total = jnp.sum(weights)
        total = jnp.where(total > 0, total, 1.0)
        left = normed(own, weights, total)
        right = normed(items[0], weights, total)
        corr = jnp.dot(left.T, right, preferred_element_type=jnp.float32)
        return jnp.sum(corr * corr, axis=1)

    return lax.map(one_slot, (other, part_w))


def slice_device(activations, routing, pairs):
    own = activations[0]
    experts = lax.axis_size("expert")
    me = lax.axis_index("expert")
    tokens = own.shape[0]
    width = own.shape[1]
    piece = tokens // experts
    columns = lax.all_to_all(
        own.reshape(experts, piece, width), "expert", split_axis=0, concat_axis=0, tiled=True
    )
    local_rows = lax.dynamic_slice_in_dim(routing, me * piece, piece, 0)
    local_table = weights_for(local_rows, experts)
    valid = (pairs >= 0).astype(jnp.float32)
    safe = jnp.maximum(pairs, 0).T
    send_blocks = columns[safe]
    send_weights = (local_table.T[safe] * valid.T[:, :, None]).astype(jnp.bfloat16)
    own_w = 0.5 + 1.5 * jnp.any(routing == me, axis=1).astype(jnp.float32)
    result = energies(
        own,
        own_w,
        lax.all_to_all(send_blocks, "expert", split_axis=1, concat_axis=1, tiled=True),
        lax.all_to_all(send_weights, "expert", split_axis=1, concat_axis=1, tiled=True),
    )
    return result[None]


def per_device(activations, routing, pairs):
    experts = lax.axis_size("expert")
    tokens, width = activations.shape[1:]
    gram_sends = experts * tokens * tokens
    slice_sends = (1 + pairs.shape[1]) * tokens * width
    if gram_sends < slice_sends:
        return gram_device(activations, routing, pairs)
    return slice_device(activations, routing, pairs)


def solution(mesh):
    return jax.shard_map(
        per_device,
        mesh=mesh,
        in_specs=(P("expert", "groups", None), P("groups", None), P()),
        out_specs=P("expert", "groups", None),
        check_vma=False,
    )
```

```python
import functools

import jax
import jax.numpy as jnp
from jax import lax
from jax.experimental import pallas as pl
from jax.experimental.pallas import tpu as pltpu
from jax.sharding import PartitionSpec as P

F32 = jnp.float32
BF16 = jnp.bfloat16
CHUNK = 256
AHEAD = 4


def gram_kernel(
    experts, order, x_hbm, routing_ref, pairs_ref, out_ref,
    x_ref, z_ref, wt_ref, send_ref, recv_ref, edge_ref, edge_in_ref, mean_ref, rate_ref,
    load_sem, send_sem, recv_sem, edge_sem, edge_in_sem,
):
    me = lax.axis_index("expert")
    tokens, width = x_ref.shape
    slots = wt_ref.shape[0]
    load = pltpu.make_async_copy(x_hbm, x_ref, load_sem)
    load.start()
    half = experts // 2 if experts % 2 == 0 else experts

    def split(index):
        upper = jnp.where(index >= half, 1, 0)
        return upper, index - upper * half

    def wrap(value, count):
        return jnp.where(value >= count, value - count, value)

    my_upper, my_place = split(me)

    def toward(s):
        upper, place = (s // half, s % half) if isinstance(s, int) else split(s)
        return wrap(my_upper + upper, 2) * half + wrap(my_place + place, half)

    def between(start, end):
        return wrap(end[0] - start[0] + 2, 2) * half + wrap(end[1] - start[1] + half, half)

    barrier = pltpu.get_barrier_semaphore()
    for s in range(1, experts):
        pl.semaphore_signal(
            barrier, inc=1, device_id={"expert": toward(s)},
            device_id_type=pl.DeviceIdType.MESH,
        )

    slot = lax.broadcasted_iota(jnp.int32, (slots, tokens), 0)
    label = toward(slot)
    hit = jnp.zeros((slots, tokens), jnp.bool_)
    mine = jnp.zeros((1, tokens), jnp.bool_)
    for k in range(routing_ref.shape[0]):
        chosen = routing_ref[k:k + 1, :]
        hit = hit | (chosen == label)
        mine = mine | (chosen == me)
    wt = jnp.where(slot == 0, 1.0, jnp.where(hit, 2.0, 0.5) * jnp.where(mine, 2.0, 0.5))
    wt_ref[...] = wt
    w = wt.T
    total = jnp.sum(wt, axis=1, keepdims=True)
    inverse = 1.0 / total
    root = jnp.sqrt(inverse)
    wt16 = wt.astype(BF16)
    wt_twice = jnp.concatenate([wt16, wt16], axis=1)

    load.wait()
    for c in range(0, width, CHUNK):
        cols = slice(c, c + CHUNK)
        x = x_ref[:, cols]
        mean = jnp.dot(wt16, x, preferred_element_type=F32) * inverse
        center = mean[0:1, :]
        y = x.astype(F32) - center
        sq = y * y
        high = sq.astype(BF16)
        low = (sq - high.astype(F32)).astype(BF16)
        second = (
            jnp.dot(wt_twice, jnp.concatenate([high, low], axis=0), preferred_element_type=F32)
        ) * inverse
        moved = mean - center
        var = jnp.maximum(second - moved * moved, 0.0)
        mean_ref[:, cols] = mean
        rate_ref[:, cols] = lax.rsqrt(var + 1e-06) * root

    mid = tokens // 2
    row = lax.broadcasted_iota(jnp.int32, (mid, tokens), 0)
    col = lax.broadcasted_iota(jnp.int32, (mid, tokens), 1)
    factor = jnp.where(row == col, 1.0, 2.0)

    arrays = (
        (send_ref, recv_ref, send_sem, recv_sem),
        (edge_ref, edge_in_ref, edge_sem, edge_in_sem),
    )

    def send(s):
        for source, target, out_sem, in_sem in arrays:
            copy = pltpu.make_async_remote_copy(
                src_ref=source.at[s],
                dst_ref=target.at[s],
                send_sem=out_sem,
                recv_sem=in_sem,
                device_id={"expert": toward(s)},
                device_id_type=pl.DeviceIdType.MESH,
            )
            copy.start()

    for n, s in enumerate(order):
        for c in range(0, width, CHUNK):
            cols = slice(c, c + CHUNK)
            z_ref[s, :, cols] = (
                (x_ref[:, cols].astype(F32) - mean_ref[s:s + 1, cols]) * rate_ref[s:s + 1, cols]
            ).astype(BF16)
        z = z_ref[s]
        gram = lax.dot_general(z, z, (((1,), (1,)), ((), ())), preferred_element_type=F32)
        gram = gram * w[:, s:s + 1] * wt_ref[s:s + 1, :]
        top = gram[:mid, :] * factor
        below = pltpu.roll(gram[mid:, :], mid, 1)
        send_ref[s] = jnp.where(row <= col, top, below * 2.0).astype(BF16)
        edge_ref[s] = jnp.sum(jnp.where(row == col, below, 0.0), axis=0, keepdims=True)
        if n + 1 == AHEAD:
            pl.semaphore_wait(barrier, experts - 1)
            for earlier in order[:n]:
                send(earlier)
        if n + 1 >= AHEAD:
            send(s)

    others = pl.ds(1, experts - 1)
    exchanges = [
        pltpu.make_async_remote_copy(
            src_ref=source.at[others],
            dst_ref=target.at[others],
            send_sem=out_sem,
            recv_sem=in_sem,
            device_id={"expert": toward(1)},
            device_id_type=pl.DeviceIdType.MESH,
        )
        for source, target, out_sem, in_sem in arrays
    ]
    for exchange in exchanges:
        exchange.wait_recv()

    for p in range(pairs_ref.shape[0]):
        partner = pairs_ref[p, me]
        used = partner >= 0
        other = jnp.where(used, partner, toward(1))
        ahead = between((my_upper, my_place), split(other))
        behind = between(split(other), (my_upper, my_place))
        packed = recv_ref[behind].astype(F32)
        edge = jnp.where(row == col, edge_in_ref[behind], 0.0)
        lower = pltpu.roll(jnp.where(row > col, packed, edge), mid, 1)
        gram = jnp.concatenate([jnp.where(row <= col, packed, 0.0), lower], axis=0).astype(BF16)
        keep = jnp.where(used, 1.0, 0.0).astype(F32)
        for c in range(0, width, CHUNK):
            cols = slice(c, c + CHUNK)
            z = z_ref[ahead, :, cols]
            product = jnp.dot(gram, z, preferred_element_type=F32)
            out_ref[p, :, cols] = jnp.sum(product * z.astype(F32), axis=0, keepdims=True) * keep

    for exchange in exchanges:
        exchange.wait_send()


def sending_order(experts):
    half = experts // 2
    far, near = list(range(half, experts)), list(range(1, half))
    return far + near


def gram_device(activations, routing, pairs):
    experts = lax.axis_size("expert")
    own = activations[0]
    tokens, width = own.shape
    count = pairs.shape[1]
    slots = -(-experts // 8) * 8
    order = sending_order(experts)
    vmem = pl.BlockSpec(memory_space=pltpu.VMEM)
    result = pl.pallas_call(
        functools.partial(gram_kernel, experts, order),
        out_shape=jax.ShapeDtypeStruct((count, 1, width), F32),
        in_specs=[pl.BlockSpec(memory_space=pltpu.HBM), vmem, pl.BlockSpec(memory_space=pltpu.SMEM)],
        out_specs=vmem,
        scratch_shapes=[
            pltpu.VMEM((tokens, width), BF16),
            pltpu.VMEM((experts, tokens, width), BF16),
            pltpu.VMEM((slots, tokens), F32),
            pltpu.VMEM((experts, tokens // 2, tokens), BF16),
            pltpu.VMEM((experts, tokens // 2, tokens), BF16),
            pltpu.VMEM((experts, 1, tokens), F32),
            pltpu.VMEM((experts, 1, tokens), F32),
            pltpu.VMEM((slots, width), F32),
            pltpu.VMEM((slots, width), F32),
            pltpu.SemaphoreType.DMA,
            pltpu.SemaphoreType.DMA,
            pltpu.SemaphoreType.DMA,
            pltpu.SemaphoreType.DMA,
            pltpu.SemaphoreType.DMA,
        ],
        compiler_params=pltpu.CompilerParams(
            collective_id=0, has_side_effects=True, vmem_limit_bytes=60 * 1024 * 1024
        ),
    )(own, routing.T, pairs.T)
    return result.reshape(1, count, width)


def weights_for(routing, experts):
    labels = jnp.arange(experts, dtype=jnp.int32)
    hit = jnp.any(routing[:, :, None] == labels[None, None, :], axis=1)
    return 0.5 + 1.5 * hit.astype(jnp.float32)


def normed(values, weights, total):
    values = values.astype(jnp.float32)
    center = jnp.sum(weights[:, None] * values, axis=0) / total
    shifted = values - center[None, :]
    spread = jnp.sum(weights[:, None] * shifted * shifted, axis=0) / total
    scale = jnp.sqrt(weights / total)[:, None]
    return (shifted * scale / jnp.sqrt(spread[None, :] + 1e-06)).astype(jnp.bfloat16)


def energies(own, own_w, blocks, partner_w):
    count = blocks.shape[0]
    tokens = own.shape[0]
    width = own.shape[1]
    other = blocks.reshape(count, tokens, width)
    part_w = partner_w.reshape(count, tokens)

    def one_slot(items):
        weights = own_w * items[1].astype(jnp.float32)
        total = jnp.sum(weights)
        total = jnp.where(total > 0, total, 1.0)
        left = normed(own, weights, total)
        right = normed(items[0], weights, total)
        corr = jnp.dot(left.T, right, preferred_element_type=jnp.float32)
        return jnp.sum(corr * corr, axis=1)

    return lax.map(one_slot, (other, part_w))


def slice_device(activations, routing, pairs):
    own = activations[0]
    experts = lax.axis_size("expert")
    me = lax.axis_index("expert")
    tokens = own.shape[0]
    width = own.shape[1]
    piece = tokens // experts
    columns = lax.all_to_all(
        own.reshape(experts, piece, width), "expert", split_axis=0, concat_axis=0, tiled=True
    )
    local_rows = lax.dynamic_slice_in_dim(routing, me * piece, piece, 0)
    local_table = weights_for(local_rows, experts)
    valid = (pairs >= 0).astype(jnp.float32)
    safe = jnp.maximum(pairs, 0).T
    send_blocks = columns[safe]
    send_weights = (local_table.T[safe] * valid.T[:, :, None]).astype(jnp.bfloat16)
    own_w = 0.5 + 1.5 * jnp.any(routing == me, axis=1).astype(jnp.float32)
    result = energies(
        own,
        own_w,
        lax.all_to_all(send_blocks, "expert", split_axis=1, concat_axis=1, tiled=True),
        lax.all_to_all(send_weights, "expert", split_axis=1, concat_axis=1, tiled=True),
    )
    return result[None]


def per_device(activations, routing, pairs):
    experts = lax.axis_size("expert")
    tokens, width = activations.shape[1:]
    gram_sends = experts * tokens * tokens
    slice_sends = (1 + pairs.shape[1]) * tokens * width
    if gram_sends < slice_sends:
        return gram_device(activations, routing, pairs)
    return slice_device(activations, routing, pairs)


def solution(mesh):
    return jax.shard_map(
        per_device,
        mesh=mesh,
        in_specs=(P("expert", "groups", None), P("groups", None), P()),
        out_specs=P("expert", "groups", None),
        check_vma=False,
    )
```
